32 devices in a mesh: row: 8 (over z, x), col: 4 (over y, core).
Axes of the slice: x: 2, y: 2, z: 4, core: 2. Of those that a mesh axis runs over, the one named last changes fastest.
Arguments:
- pair: bfloat16 [128, 128, 128], P('row', 'col'), may hold values from -6 to 6
- norm_gain: float32 [128], replicated, may hold values from 0.1 to 1.9
- norm_shift: float32 [128], replicated, may hold values from -3 to 3
- tri_weight: bfloat16 [128, 640], replicated, may hold values from -0.5 to 0.5
- tri_out_gain: float32 [128], replicated, may hold values from 0.1 to 1.9
- tri_out_shift: float32 [128], replicated, may hold values from -3 to 3
- tri_out_weight: bfloat16 [128, 128], replicated, may hold values from -0.5 to 0.5
- att_gain: float32 [128], replicated, may hold values from 0.1 to 1.9
- att_shift: float32 [128], replicated, may hold values from -3 to 3
- att_weight: bfloat16 [128, 512], replicated, may hold values from -0.5 to 0.5
- bias_weight: bfloat16 [128, 4], replicated, may hold values from -12 to 12
- att_out_weight: bfloat16 [128, 128], replicated, may hold values from -0.5 to 0.5
Outputs:
- pair_mid: bfloat16 [128, 128, 128], P('row', 'col')
- pair_out: bfloat16 [128, 128, 128], P('row', 'col')
The draws below stay inside these ranges and needn't reach their ends.
All inputs are finite; a program needn't handle non-finite values.
Results may differ from the reference program's by a relative error of at most 0.014.
Values may be sent and summed in bfloat16 or wider, within the bound.
A program may use at most 128 MiB of HBM per device.

```python
import jax
import jax.numpy as jnp
from jax import lax

C = 128
HT = 128
H = 4
DH = 32
N = 128


def draw_bias_weight(key, part):
    key = jax.random.fold_in(key, 11)
    base_key, scale_key = jax.random.split(key)
    base = jnp.clip(jax.random.normal(base_key, (C, H), jnp.float32), -3.0, 3.0)
    low, high = (0.7, 2.5)
    scales = jnp.exp(jax.random.uniform(scale_key, (1, H), jnp.float32, jnp.log(low), jnp.log(high)))
    return (base * 0.1 * scales).astype(jnp.bfloat16)


def steps_of(rng, extent, shards, low, largest):
    def one(axis_at, parts):
        heights = jax.random.uniform(jax.random.fold_in(jax.random.fold_in(rng, 6), axis_at), (parts,), jnp.float32, low / len(shards), largest / len(shards))
        return jnp.repeat(jnp.exp(heights), extent[axis_at] // parts).reshape((-1,) + (1,) * (len(extent) - axis_at - 1))

    loudness = one(*shards[0])
    for cut in shards[1:]:
        loudness = loudness * one(*cut)
    return loudness


def noise(rng, dims, scale, limit, cuts=(), kind=jnp.bfloat16):
    values = scale * jax.random.normal(rng, dims, jnp.float32)
    if cuts:
        values = values * steps_of(rng, dims, cuts, -0.22, 0.18)
    return jnp.clip(values, -limit, limit).astype(kind)


def setup_inputs(seed: int = 0) -> dict:
    splits = jax.random.split(jax.random.key(seed), 13)
    pair = noise(splits[0], (N, N, C), 1.0, 6.0, ((0, 8), (1, 4)))
    norm_gain = jnp.clip(1.0 + 0.18 * jax.random.normal(splits[1], (C,), jnp.float32), 0.1, 1.9)
    norm_shift = noise(splits[2], (C,), 0.5, 3.0, (), jnp.float32)
    tri_weight = noise(splits[3], (C, 4 * HT + C), C ** -0.5, 0.5)
    tri_out_gain = jnp.clip(1.0 + 0.18 * jax.random.normal(splits[4], (HT,), jnp.float32), 0.1, 1.9)
    tri_out_shift = noise(splits[5], (HT,), 0.5, 3.0, (), jnp.float32)
    tri_out_weight = noise(splits[6], (HT, C), HT ** -0.5, 0.5)
    att_gain = jnp.clip(1.0 + 0.18 * jax.random.normal(splits[7], (C,), jnp.float32), 0.1, 1.9)
    att_shift = noise(splits[8], (C,), 0.5, 3.0, (), jnp.float32)
    att_weight = noise(splits[9], (C, 4 * H * DH), C ** -0.5, 0.5)
    bias_weight = draw_bias_weight(jax.random.fold_in(splits[12], 71), 0)
    att_out_weight = noise(splits[11], (H * DH, C), (H * DH) ** -0.5, 0.5)
    return dict(pair=pair, norm_gain=norm_gain, norm_shift=norm_shift, tri_weight=tri_weight, tri_out_gain=tri_out_gain, tri_out_shift=tri_out_shift, tri_out_weight=tri_out_weight, att_gain=att_gain, att_shift=att_shift, att_weight=att_weight, bias_weight=bias_weight, att_out_weight=att_out_weight)


eps = 1e-05

def normalize(values, gain, shift):
    mean = lax.optimization_barrier(jnp.mean(values, axis=-1, keepdims=True))
    centred = values - mean
    spread = lax.optimization_barrier(jnp.mean(centred * centred, axis=-1, keepdims=True))
    return centred * lax.rsqrt(spread + eps) * gain + shift

def reference(pair, norm_gain, norm_shift, tri_weight, tri_out_gain, tri_out_shift, tri_out_weight, att_gain, att_shift, att_weight, bias_weight, att_out_weight):
    residues = pair.shape[0]
    hidden = tri_out_weight.shape[0]
    heads = bias_weight.shape[1]
    inner = att_out_weight.shape[0]
    head_dim = inner // heads
    normed = normalize(pair.astype(jnp.float32), norm_gain, norm_shift).astype(jnp.bfloat16)
    proj = jnp.dot(normed, tri_weight, preferred_element_type=jnp.float32)
    left = (jax.nn.sigmoid(proj[..., :hidden]) * proj[..., hidden:2 * hidden]).astype(jnp.bfloat16)
    right = (jax.nn.sigmoid(proj[..., 2 * hidden:3 * hidden]) * proj[..., 3 * hidden:4 * hidden]).astype(jnp.bfloat16)
    out_gate = proj[..., 4 * hidden:]
    edges = jnp.einsum('ikh,jkh->ijh', left.astype(jnp.float32), right.astype(jnp.float32), precision=lax.Precision.HIGHEST)
    tri_normed = normalize(edges, tri_out_gain, tri_out_shift).astype(jnp.bfloat16)
    update = jnp.dot(tri_normed, tri_out_weight, preferred_element_type=jnp.float32)
    pair_mid = (pair.astype(jnp.float32) + jax.nn.sigmoid(out_gate) * update).astype(jnp.bfloat16)
    att_in = normalize(pair_mid.astype(jnp.float32), att_gain, att_shift).astype(jnp.bfloat16)
    proj2 = jnp.dot(att_in, att_weight, preferred_element_type=jnp.float32)
    query = (proj2[..., :inner] * head_dim ** (-0.5)).astype(jnp.bfloat16)
    key = proj2[..., inner:2 * inner].astype(jnp.bfloat16)
    value = proj2[..., 2 * inner:3 * inner].astype(jnp.bfloat16)
    att_gate = proj2[..., 3 * inner:]
    bias = jnp.einsum('xyd,dh->hxy', att_in.astype(jnp.float32), bias_weight.astype(jnp.float32), precision=lax.Precision.HIGHEST).astype(jnp.bfloat16)
    bias_turned = jnp.transpose(bias, (0, 2, 1)).astype(jnp.float32)

    def column(index):
        q_col = lax.dynamic_index_in_dim(query, index, 1, keepdims=False).astype(jnp.float32).reshape(residues, heads, head_dim)
        k_col = lax.dynamic_index_in_dim(key, index, 1, keepdims=False).astype(jnp.float32).reshape(residues, heads, head_dim)
        v_col = lax.dynamic_index_in_dim(value, index, 1, keepdims=False).astype(jnp.float32).reshape(residues, heads, head_dim)
        scores = jnp.einsum('ihd,khd->hik', q_col, k_col, precision=lax.Precision.HIGHEST) + bias_turned
        top = lax.optimization_barrier(jnp.max(scores, axis=-1, keepdims=True))
        expd = jnp.exp(scores - top)
        total = lax.optimization_barrier(jnp.sum(expd, axis=-1))
        weights = expd.astype(jnp.bfloat16).astype(jnp.float32)
        mixed = jnp.einsum('hik,khd->hid', weights, v_col, precision=lax.Precision.HIGHEST) / total[..., None]
        return jnp.transpose(mixed, (1, 0, 2)).reshape(residues, inner)
    attended = lax.map(column, jnp.arange(residues, dtype=jnp.int32))
    attended = jnp.transpose(attended, (1, 0, 2))
    gated = (attended * jax.nn.sigmoid(att_gate)).astype(jnp.bfloat16)
    pair_out = (pair_mid.astype(jnp.float32) + jnp.dot(gated, att_out_weight, preferred_element_type=jnp.float32)).astype(jnp.bfloat16)
    return (pair_mid, pair_out)
```

```python
import functools

import jax
import jax.numpy as jnp
from jax import lax
from jax.experimental import pallas as pl
from jax.experimental.pallas import tpu as pltpu
from jax.sharding import PartitionSpec as P

eps = 1e-05
f32 = jnp.float32
bf16 = jnp.bfloat16
MESH = pl.DeviceIdType.MESH
NT = (((1,), (1,)), ((), ()))
TN = (((0,), (0,)), ((), ()))


def normalize(values, gain, shift):
    mean = jnp.mean(values, axis=-1, keepdims=True)
    centred = values - mean
    spread = jnp.mean(centred * centred, axis=-1, keepdims=True)
    return centred * lax.rsqrt(spread + eps) * gain + shift


def same_group(rows, lanes, row_size, lane_size):
    row = lax.div(lax.broadcasted_iota(jnp.int32, (rows, lanes), 0), jnp.int32(row_size))
    lane = lax.div(lax.broadcasted_iota(jnp.int32, (rows, lanes), 1), jnp.int32(lane_size))
    return row == lane


def kernel(
    R, C,
    pair_ref, ng_ref, ns_ref, tw_ref, tg_ref, ts_ref, tow_ref, ag_ref, as_ref, aw_ref, bw_ref, aow_ref,
    mid_ref, out_ref,
    scr, gate_scr, send_a, recv_a, send_b, recv_b, send_d, recv_d, send_bias, recv_bias, send_f, recv_f,
    ssem_a, rsem_a, ssem_b, rsem_b, ssem_d, rsem_d, ssem_bias, rsem_bias, ssem_f, rsem_f,
):
    D = R * C
    rows, cols, width = pair_ref.shape
    hidden = tow_ref.shape[0]
    heads = bw_ref.shape[1]
    inner = aow_ref.shape[0]
    head_dim = inner // heads
    places = rows * cols
    residues = R * rows
    per = hidden // D
    lanes = per * cols
    share = cols // R
    r, c = lax.axis_index("row"), lax.axis_index("col")
    me = r * C + c

    barrier = pltpu.get_barrier_semaphore()

    def greet(s, _):
        t = lax.rem(me + s, D)
        pl.semaphore_signal(
            barrier, inc=1, device_id=(lax.div(t, C), lax.rem(t, C)), device_id_type=MESH
        )
        return _

    lax.fori_loop(1, D, greet, 0)

    x = pair_ref[...].astype(f32).reshape(places, width)
    normed = normalize(x, ng_ref[...], ns_ref[...]).astype(bf16)

    def spread_channels(side):
        at = 2 * hidden * side
        gate = lax.dot_general(
            tw_ref[:, at : at + hidden], normed, (((0,), (1,)), ((), ())), preferred_element_type=f32
        )
        value = lax.dot_general(
            tw_ref[:, at + hidden : at + 2 * hidden], normed, (((0,), (1,)), ((), ())),
            preferred_element_type=f32,
        )
        turned = jax.nn.sigmoid(gate) * value
        for i in range(rows):
            pieces = [
                turned[h * D : (h + 1) * D, i * cols : (i + 1) * cols] for h in range(per)
            ]
            scr[pl.ds(i, D, stride=rows), :] = jnp.concatenate(pieces, axis=1)
        send_a[:, side] = scr[...].astype(bf16).reshape(D, rows, lanes)

    spread_channels(0)
    spread_channels(1)

    pl.semaphore_wait(barrier, D - 1)

    def copy_a(s, target, source):
        return pltpu.make_async_remote_copy(
            src_ref=send_a.at[target], dst_ref=recv_a.at[lax.rem(source, C), lax.div(source, C)],
            send_sem=ssem_a.at[s], recv_sem=rsem_a.at[s],
            device_id=(lax.div(target, C), lax.rem(target, C)), device_id_type=MESH,
        )

    def copy_b(s, target, source):
        return pltpu.make_async_remote_copy(
            src_ref=send_b.at[lax.rem(target, C), lax.div(target, C)], dst_ref=recv_b.at[source],
            send_sem=ssem_b.at[s], recv_sem=rsem_b.at[s],
            device_id=(lax.div(target, C), lax.rem(target, C)), device_id_type=MESH,
        )

    def copy_bias(s, target, source):
        return pltpu.make_async_remote_copy(
            src_ref=send_bias, dst_ref=recv_bias.at[lax.rem(source, C), lax.div(source, C)],
            send_sem=ssem_bias.at[s], recv_sem=rsem_bias.at[s],
            device_id=(lax.div(target, C), lax.rem(target, C)), device_id_type=MESH,
        )

    def copy_d(s, target, source):
        return pltpu.make_async_remote_copy(
            src_ref=send_d.at[target], dst_ref=recv_d.at[source],
            send_sem=ssem_d.at[s], recv_sem=rsem_d.at[s],
            device_id=(target, c), device_id_type=MESH,
        )

    def copy_f(s, target, source):
        return pltpu.make_async_remote_copy(
            src_ref=send_f.at[target], dst_ref=recv_f.at[source],
            send_sem=ssem_f.at[s], recv_sem=rsem_f.at[s],
            device_id=(target, c), device_id_type=MESH,
        )

    def start_all(copy, here, count):
        def body(s, _):
            copy(s, lax.rem(here + s, count), here).start()
            return _

        lax.fori_loop(1, count, body, 0)

    def arrive_all(copy, here, count):
        def body(s, _):
            copy(s, here, lax.rem(here + count - s, count)).wait_recv()
            return _

        lax.fori_loop(1, count, body, 0)

    def leave_all(copy, here, count):
        def body(s, _):
            copy(s, lax.rem(here + s, count), here).wait_send()
            return _

        lax.fori_loop(1, count, body, 0)

    start_all(copy_a, me, D)
    recv_a[c, r] = send_a[me]
    gate_scr[...] = jax.nn.sigmoid(
        jnp.dot(normed, tw_ref[:, 4 * hidden :], preferred_element_type=f32)
    )
    arrive_all(copy_a, me, D)

    left = jnp.concatenate([recv_a[k, :, 0].reshape(residues, lanes) for k in range(C)], axis=1)
    own_channel = jnp.concatenate([same_group(lanes, lanes, cols, cols)] * C, axis=1)
    for b in range(C):
        block = jnp.concatenate(
            [recv_a[k, :, 1].reshape(residues, lanes)[b * cols : (b + 1) * cols] for k in range(C)],
            axis=1,
        )
        block = jnp.where(own_channel, jnp.concatenate([block] * per, axis=0).astype(f32), 0.0)
        edges = lax.dot_general(left, block.astype(bf16), NT, preferred_element_type=f32)
        send_b[b] = edges.reshape(R, rows, lanes).astype(send_b.dtype)
    start_all(copy_b, me, D)
    recv_b[me] = send_b[c, r]
    arrive_all(copy_b, me, D)

    def over_groups(v):
        total = v
        for h in range(1, per):
            total = total + pltpu.roll(v, h * cols, 1)
        return total

    edges = recv_b[...].astype(f32)
    mean = over_groups(jnp.sum(edges, axis=0)) * (1.0 / hidden)
    centred = edges - mean[None]
    spread = over_groups(jnp.sum(centred * centred, axis=0)) * (1.0 / hidden)
    scaled = centred * lax.rsqrt(spread + eps)[None]
    scr[...] = scaled.reshape(D * rows, lanes)
    gathered = []
    for i in range(rows):
        turned = scr[pl.ds(i, D, stride=rows), :].T
        gathered.append(
            jnp.concatenate([turned[h * cols : (h + 1) * cols] for h in range(per)], axis=1)
        )
    tri_normed = (jnp.concatenate(gathered, axis=0) * tg_ref[...] + ts_ref[...]).astype(bf16)
    update = jnp.dot(tri_normed, tow_ref[...], preferred_element_type=f32)
    x = pair_ref[...].astype(f32).reshape(places, width)
    mid = (x + gate_scr[...] * update).astype(bf16)
    mid_ref[...] = mid.reshape(rows, cols, width)

    att_in = normalize(mid.astype(f32), ag_ref[...], as_ref[...]).astype(bf16).astype(f32)
    for i in range(rows):
        gate_scr[pl.ds(i, cols, stride=rows), :] = att_in[i * cols : (i + 1) * cols]
    att_t = gate_scr[...].astype(bf16)
    send_d[...] = att_t.reshape(R, share, rows, width)
    start_all(copy_d, r, R)
    wide = heads * cols
    spread_bw = jnp.concatenate(
        [
            jnp.broadcast_to(bw_ref[:, h : h + 1].astype(f32), (width, cols))
            for h in range(heads)
        ],
        axis=1,
    ).astype(bf16)
    products = jnp.dot(att_t, spread_bw, preferred_element_type=f32).reshape(cols, rows, wide)
    lane_col = lax.rem(lax.broadcasted_iota(jnp.int32, (rows, wide), 1), jnp.int32(cols))
    bias = jnp.zeros((rows, wide), f32)
    for y in range(cols):
        bias = jnp.where(lane_col == y, products[y], bias)
    send_bias[...] = bias.astype(bf16)
    start_all(copy_bias, me, D)
    recv_d[r] = send_d[r]
    recv_bias[c, r] = send_bias[...]
    arrive_all(copy_d, r, R)

    columns = [recv_d[:, j].reshape(residues, width) for j in range(share)]
    own_head = same_group(wide, inner, cols, head_dim)
    projected = [jnp.dot(a, aw_ref[...], preferred_element_type=f32) for a in columns]
    arrive_all(copy_bias, me, D)
    for j in range(share):
        proj = projected[j]
        query = (proj[:, :inner] * head_dim ** (-0.5)).astype(bf16).astype(f32)
        key = proj[:, inner : 2 * inner].astype(bf16)
        value = proj[:, 2 * inner : 3 * inner].astype(bf16)
        gate = jax.nn.sigmoid(proj[:, 3 * inner :])
        mixed = []
        for b in range(C):
            tiled = jnp.concatenate([query[b * cols : (b + 1) * cols]] * heads, axis=0)
            tiled = jnp.where(own_head, tiled, 0.0).astype(bf16)
            scores = lax.dot_general(key, tiled, NT, preferred_element_type=f32)
            scores = scores + recv_bias[b].reshape(residues, wide).astype(f32)
            top = jnp.max(scores, axis=0, keepdims=True)
            expd = jnp.exp(scores - top)
            total = jnp.sum(expd, axis=0, keepdims=True)
            weights = (expd * (1.0 / total)).astype(bf16)
            full = lax.dot_general(weights, value, TN, preferred_element_type=f32)
            full = jnp.where(own_head, full, 0.0)
            part = full[:cols]
            for h in range(1, heads):
                part = part + full[h * cols : (h + 1) * cols]
            mixed.append(part)
        gated = (jnp.concatenate(mixed, axis=0) * gate).astype(bf16)
        send_f[:, j] = gated.reshape(R, rows, inner)
    start_all(copy_f, r, R)
    recv_f[r] = send_f[r]
    leave_all(copy_a, me, D)
    leave_all(copy_b, me, D)
    leave_all(copy_d, r, R)
    leave_all(copy_bias, me, D)
    arrive_all(copy_f, r, R)
    final = jnp.dot(
        recv_f[...].reshape(places, inner), aow_ref[...], preferred_element_type=f32
    )
    for j in range(cols):
        gate_scr[pl.ds(j, rows, stride=cols), :] = final[j * rows : (j + 1) * rows]
    out = mid_ref[...].astype(f32).reshape(places, width) + gate_scr[...]
    out_ref[...] = out.astype(bf16).reshape(rows, cols, width)
    leave_all(copy_f, r, R)


def local(R, C, pair, ng, ns, tw, tg, ts, tow, ag, ash, aw, bw, aow):
    rows, cols, width = pair.shape
    D = R * C
    hidden = tow.shape[0]
    heads = bw.shape[1]
    inner = aow.shape[0]
    lanes = hidden // D * cols
    share = cols // R
    wide = heads * cols
    places = rows * cols
    vmem = pl.BlockSpec(memory_space=pltpu.VMEM)
    dma = pltpu.SemaphoreType.DMA
    return pl.pallas_call(
        functools.partial(kernel, R, C),
        out_shape=(
            jax.ShapeDtypeStruct(pair.shape, bf16),
            jax.ShapeDtypeStruct(pair.shape, bf16),
        ),
        in_specs=[vmem] * 12,
        out_specs=(vmem, vmem),
        scratch_shapes=[
            pltpu.VMEM((D * rows, lanes), f32),
            pltpu.VMEM((places, width), f32),
            pltpu.VMEM((D, 2, rows, lanes), bf16),
            pltpu.VMEM((C, R, 2, rows, lanes), bf16),
            pltpu.VMEM((C, R, rows, lanes), f32),
            pltpu.VMEM((D, rows, lanes), f32),
            pltpu.VMEM((R, share, rows, width), bf16),
            pltpu.VMEM((R, share, rows, width), bf16),
            pltpu.VMEM((rows, wide), bf16),
            pltpu.VMEM((C, R, rows, wide), bf16),
            pltpu.VMEM((R, share, rows, inner), bf16),
            pltpu.VMEM((R, share, rows, inner), bf16),
            dma((D,)), dma((D,)), dma((D,)), dma((D,)), dma((R,)), dma((R,)),
            dma((D,)), dma((D,)), dma((R,)), dma((R,)),
        ],
        compiler_params=pltpu.CompilerParams(
            collective_id=0, has_side_effects=True, vmem_limit_bytes=48 * 1024 * 1024
        ),
    )(pair, ng[None], ns[None], tw, tg[None], ts[None], tow, ag[None], ash[None], aw, bw, aow)


def solution(mesh):
    R, C = mesh.shape["row"], mesh.shape["col"]
    return jax.shard_map(
        functools.partial(local, R, C),
        mesh=mesh,
        in_specs=(P("row", "col", None), P(), P(), P(), P(), P(), P(), P(), P(), P(), P(), P()),
        out_specs=(P("row", "col", None), P("row", "col", None)),
        check_vma=False,
    )
```

```python
import functools

import jax
import jax.numpy as jnp
from jax import lax
from jax.experimental import pallas as pl
from jax.experimental.pallas import tpu as pltpu
from jax.sharding import PartitionSpec as P

eps = 1e-05
f32 = jnp.float32
bf16 = jnp.bfloat16
MESH = pl.DeviceIdType.MESH
NT = (((1,), (1,)), ((), ()))
TN = (((0,), (0,)), ((), ()))


def normalize(values, gain, shift):
    mean = jnp.mean(values, axis=-1, keepdims=True)
    centred = values - mean
    spread = jnp.mean(centred * centred, axis=-1, keepdims=True)
    return centred * lax.rsqrt(spread + eps) * gain + shift


def same_group(rows, lanes, row_size, lane_size):
    row = lax.div(lax.broadcasted_iota(jnp.int32, (rows, lanes), 0), jnp.int32(row_size))
    lane = lax.div(lax.broadcasted_iota(jnp.int32, (rows, lanes), 1), jnp.int32(lane_size))
    return row == lane


def kernel(
    R, C,
    pair_hbm, ng_hbm, ns_hbm, tw_hbm, tg_hbm, ts_hbm, tow_hbm, ag_hbm, as_hbm, aw_hbm, bw_hbm, aow_hbm,
    mid_ref, out_ref,
    pair_ref, ng_ref, ns_ref, tw_ref, tg_ref, ts_ref, tow_ref, ag_ref, as_ref, aw_ref, bw_ref, aow_ref,
    fetch_sem,
    scr, gate_scr, send_a, recv_a, send_b, recv_b, send_d, recv_d, send_bias, recv_bias, send_f, recv_f,
    ssem_a, rsem_a, ssem_b, rsem_b, ssem_d, rsem_d, ssem_bias, rsem_bias, ssem_f, rsem_f,
):
    D = R * C
    rows, cols, width = pair_ref.shape
    hidden = tow_ref.shape[0]
    heads = bw_ref.shape[0]
    inner = aow_ref.shape[0]
    head_dim = inner // heads
    places = rows * cols
    residues = R * rows
    per = hidden // D
    lanes = per * cols
    share = cols // R
    parts, _, chunk = send_f.shape[:3]
    r, c = lax.axis_index("row"), lax.axis_index("col")
    me = r * C + c

    barrier = pltpu.get_barrier_semaphore()

    def greet(s, _):
        t = lax.rem(me + s, D)
        pl.semaphore_signal(
            barrier, inc=1, device_id=(lax.div(t, C), lax.rem(t, C)), device_id_type=MESH
        )
        return _

    lax.fori_loop(1, D, greet, 0)

    fetches = [
        pltpu.make_async_copy(source, target, fetch_sem.at[n])
        for n, (source, target) in enumerate(
            [
                (pair_hbm, pair_ref), (ng_hbm, ng_ref), (ns_hbm, ns_ref), (tw_hbm, tw_ref),
                (tg_hbm, tg_ref), (ts_hbm, ts_ref), (tow_hbm, tow_ref), (ag_hbm, ag_ref),
                (as_hbm, as_ref), (aw_hbm, aw_ref), (bw_hbm, bw_ref), (aow_hbm, aow_ref),
            ]
        )
    ]
    for fetch in fetches:
        fetch.start()
    for fetch in fetches[:4]:
        fetch.wait()

    x = pair_ref[...].astype(f32).reshape(places, width)
    normed = normalize(x, ng_ref[...], ns_ref[...]).astype(bf16)

    def spread_channels(side):
        at = 2 * hidden * side
        gate = lax.dot_general(
            tw_ref[:, at : at + hidden], normed, (((0,), (1,)), ((), ())), preferred_element_type=f32
        )
        value = lax.dot_general(
            tw_ref[:, at + hidden : at + 2 * hidden], normed, (((0,), (1,)), ((), ())),
            preferred_element_type=f32,
        )
        turned = jax.nn.sigmoid(gate) * value
        for i in range(rows):
            pieces = [
                turned[h * D : (h + 1) * D, i * cols : (i + 1) * cols] for h in range(per)
            ]
            scr[pl.ds(i, D, stride=rows), :] = jnp.concatenate(pieces, axis=1)
        send_a[:, side] = scr[...].astype(bf16).reshape(D, rows, lanes)

    spread_channels(0)
    spread_channels(1)

    pl.semaphore_wait(barrier, D - 1)

    def copy_a(s, target, source):
        return pltpu.make_async_remote_copy(
            src_ref=send_a.at[target], dst_ref=recv_a.at[lax.rem(source, C), lax.div(source, C)],
            send_sem=ssem_a.at[s], recv_sem=rsem_a.at[s],
            device_id=(lax.div(target, C), lax.rem(target, C)), device_id_type=MESH,
        )

    def copy_b(s, target, source):
        return pltpu.make_async_remote_copy(
            src_ref=send_b.at[lax.rem(target, C), lax.div(target, C)], dst_ref=recv_b.at[source],
            send_sem=ssem_b.at[s], recv_sem=rsem_b.at[s],
            device_id=(lax.div(target, C), lax.rem(target, C)), device_id_type=MESH,
        )

    def copy_bias(s, target, source):
        return pltpu.make_async_remote_copy(
            src_ref=send_bias, dst_ref=recv_bias.at[lax.rem(source, C), lax.div(source, C)],
            send_sem=ssem_bias.at[s], recv_sem=rsem_bias.at[s],
            device_id=(lax.div(target, C), lax.rem(target, C)), device_id_type=MESH,
        )

    def copy_d(s, target, source):
        return pltpu.make_async_remote_copy(
            src_ref=send_d.at[target], dst_ref=recv_d.at[source],
            send_sem=ssem_d.at[s], recv_sem=rsem_d.at[s],
            device_id=(target, c), device_id_type=MESH,
        )

    def copy_f(part, s, target, source):
        return pltpu.make_async_remote_copy(
            src_ref=send_f.at[part, target], dst_ref=recv_f.at[part, source],
            send_sem=ssem_f.at[part * R + s], recv_sem=rsem_f.at[part * R + s],
            device_id=(target, c), device_id_type=MESH,
        )

    def start_all(copy, here, count):
        def body(s, _):
            copy(s, lax.rem(here + s, count), here).start()
            return _

        lax.fori_loop(1, count, body, 0)

    def arrive_all(copy, here, count):
        def body(s, _):
            copy(s, here, lax.rem(here + count - s, count)).wait_recv()
            return _

        lax.fori_loop(1, count, body, 0)

    def leave_all(copy, here, count):
        def body(s, _):
            copy(s, lax.rem(here + s, count), here).wait_send()
            return _

        lax.fori_loop(1, count, body, 0)

    start_all(copy_a, me, D)
    recv_a[c, r] = send_a[me]
    gate_scr[...] = jax.nn.sigmoid(
        jnp.dot(normed, tw_ref[:, 4 * hidden :], preferred_element_type=f32)
    )
    for fetch in fetches[4:]:
        fetch.wait()
    arrive_all(copy_a, me, D)

    left = jnp.concatenate([recv_a[k, :, 0].reshape(residues, lanes) for k in range(C)], axis=1)
    own_channel = jnp.concatenate([same_group(lanes, lanes, cols, cols)] * C, axis=1)
    for b in range(C):
        block = jnp.concatenate(
            [recv_a[k, :, 1].reshape(residues, lanes)[b * cols : (b + 1) * cols] for k in range(C)],
            axis=1,
        )
        block = jnp.where(own_channel, jnp.concatenate([block] * per, axis=0).astype(f32), 0.0)
        edges = lax.dot_general(left, block.astype(bf16), NT, preferred_element_type=f32)
        send_b[b] = edges.reshape(R, rows, lanes).astype(send_b.dtype)
    start_all(copy_b, me, D)
    recv_b[me] = send_b[c, r]
    arrive_all(copy_b, me, D)

    def over_groups(v):
        total = v
        for h in range(1, per):
            total = total + pltpu.roll(v, h * cols, 1)
        return total

    edges = recv_b[...].astype(f32)
    mean = over_groups(jnp.sum(edges, axis=0)) * (1.0 / hidden)
    centred = edges - mean[None]
    spread = over_groups(jnp.sum(centred * centred, axis=0)) * (1.0 / hidden)
    scaled = centred * lax.rsqrt(spread + eps)[None]
    scr[...] = scaled.reshape(D * rows, lanes)
    gathered = []
    for i in range(rows):
        turned = scr[pl.ds(i, D, stride=rows), :].T
        gathered.append(
            jnp.concatenate([turned[h * cols : (h + 1) * cols] for h in range(per)], axis=1)
        )
    tri_normed = (jnp.concatenate(gathered, axis=0) * tg_ref[...] + ts_ref[...]).astype(bf16)
    update = jnp.dot(tri_normed, tow_ref[...], preferred_element_type=f32)
    x = pair_ref[...].astype(f32).reshape(places, width)
    mid = (x + gate_scr[...] * update).astype(bf16)
    mid_ref[...] = mid.reshape(rows, cols, width)

    att_in = normalize(mid.astype(f32), ag_ref[...], as_ref[...]).astype(bf16).astype(f32)
    for i in range(rows):
        gate_scr[pl.ds(i, cols, stride=rows), :] = att_in[i * cols : (i + 1) * cols]
    att_t = gate_scr[...].astype(bf16)
    send_d[...] = att_t.reshape(R, share, rows, width)
    start_all(copy_d, r, R)
    wide = heads * cols
    spread_bw = jnp.concatenate(
        [
            jnp.broadcast_to(bw_ref[...].astype(f32)[h : h + 1], (cols, width))
            for h in range(heads)
        ],
        axis=0,
    ).astype(bf16)
    products = lax.dot_general(att_t, spread_bw, NT, preferred_element_type=f32)
    products = products.reshape(cols, rows, wide)
    lane_col = lax.rem(lax.broadcasted_iota(jnp.int32, (rows, wide), 1), jnp.int32(cols))
    bias = jnp.zeros((rows, wide), f32)
    for y in range(cols):
        bias = jnp.where(lane_col == y, products[y], bias)
    send_bias[...] = bias.astype(bf16)
    start_all(copy_bias, me, D)
    recv_d[r] = send_d[r]
    recv_bias[c, r] = send_bias[...]
    arrive_all(copy_d, r, R)

    columns = [recv_d[:, j].reshape(residues, width) for j in range(share)]
    own_head = same_group(wide, inner, cols, head_dim)
    projected = [jnp.dot(a, aw_ref[...], preferred_element_type=f32) for a in columns]
    arrive_all(copy_bias, me, D)
    for j in range(share):
        proj = projected[j]
        query = (proj[:, :inner] * head_dim ** (-0.5)).astype(bf16).astype(f32)
        key = proj[:, inner : 2 * inner].astype(bf16)
        value = proj[:, 2 * inner : 3 * inner].astype(bf16)
        gate = jax.nn.sigmoid(proj[:, 3 * inner :])
        mixed = []
        for b in range(C):
            tiled = jnp.concatenate([query[b * cols : (b + 1) * cols]] * heads, axis=0)
            tiled = jnp.where(own_head, tiled, 0.0).astype(bf16)
            scores = lax.dot_general(key, tiled, NT, preferred_element_type=f32)
            scores = scores + recv_bias[b].reshape(residues, wide).astype(f32)
            top = jnp.max(scores, axis=0, keepdims=True)
            expd = jnp.exp(scores - top)
            total = jnp.sum(expd, axis=0, keepdims=True)
            weights = (expd * (1.0 / total)).astype(bf16)
            full = lax.dot_general(weights, value, TN, preferred_element_type=f32)
            full = jnp.where(own_head, full, 0.0)
            part = full[:cols]
            for h in range(1, heads):
                part = part + full[h * cols : (h + 1) * cols]
            mixed.append(part)
        gated = (jnp.concatenate(mixed, axis=0) * gate).astype(bf16)
        part, at = j // chunk, j % chunk
        send_f[part, :, at] = gated.reshape(R, rows, inner)
        if at == chunk - 1:
            start_all(functools.partial(copy_f, part), r, R)
            recv_f[part, r] = send_f[part, r]
    leave_all(copy_a, me, D)
    leave_all(copy_b, me, D)
    leave_all(copy_d, r, R)
    leave_all(copy_bias, me, D)
    for part in range(parts):
        arrive_all(functools.partial(copy_f, part), r, R)
        final = jnp.dot(
            recv_f[part].reshape(R * chunk * rows, inner), aow_ref[...], preferred_element_type=f32
        )
        for n in range(R * chunk):
            j = n // chunk * share + part * chunk + n % chunk
            gate_scr[pl.ds(j, rows, stride=cols), :] = final[n * rows : (n + 1) * rows]
    out = mid_ref[...].astype(f32).reshape(places, width) + gate_scr[...]
    out_ref[...] = out.astype(bf16).reshape(rows, cols, width)
    for part in range(parts):
        leave_all(functools.partial(copy_f, part), r, R)


def local(R, C, pair, ng, ns, tw, tg, ts, tow, ag, ash, aw, bw, aow):
    rows, cols, width = pair.shape
    D = R * C
    hidden = tow.shape[0]
    heads = bw.shape[1]
    parts = 2 if cols // R % 2 == 0 else 1
    inner = aow.shape[0]
    lanes = hidden // D * cols
    share = cols // R
    wide = heads * cols
    places = rows * cols
    vmem = pl.BlockSpec(memory_space=pltpu.VMEM)
    dma = pltpu.SemaphoreType.DMA
    operands = (pair, ng[None], ns[None], tw, tg[None], ts[None], tow, ag[None], ash[None], aw, bw.T, aow)
    return pl.pallas_call(
        functools.partial(kernel, R, C),
        out_shape=(
            jax.ShapeDtypeStruct(pair.shape, bf16),
            jax.ShapeDtypeStruct(pair.shape, bf16),
        ),
        in_specs=[pl.BlockSpec(memory_space=pl.ANY)] * 12,
        out_specs=(vmem, vmem),
        scratch_shapes=[pltpu.VMEM(v.shape, v.dtype) for v in operands]
        + [
            dma((12,)),
            pltpu.VMEM((D * rows, lanes), f32),
            pltpu.VMEM((places, width), f32),
            pltpu.VMEM((D, 2, rows, lanes), bf16),
            pltpu.VMEM((C, R, 2, rows, lanes), bf16),
            pltpu.VMEM((C, R, rows, lanes), bf16),
            pltpu.VMEM((D, rows, lanes), bf16),
            pltpu.VMEM((R, share, rows, width), bf16),
            pltpu.VMEM((R, share, rows, width), bf16),
            pltpu.VMEM((rows, wide), bf16),
            pltpu.VMEM((C, R, rows, wide), bf16),
            pltpu.VMEM((parts, R, share // parts, rows, inner), bf16),
            pltpu.VMEM((parts, R, share // parts, rows, inner), bf16),
            dma((D,)), dma((D,)), dma((D,)), dma((D,)), dma((R,)), dma((R,)),
            dma((D,)), dma((D,)), dma((parts * R,)), dma((parts * R,)),
        ],
        compiler_params=pltpu.CompilerParams(
            collective_id=0, has_side_effects=True, vmem_limit_bytes=63 * 1024 * 1024
        ),
    )(*operands)


def solution(mesh):
    R, C = mesh.shape["row"], mesh.shape["col"]
    return jax.shard_map(
        functools.partial(local, R, C),
        mesh=mesh,
        in_specs=(P("row", "col", None), P(), P(), P(), P(), P(), P(), P(), P(), P(), P(), P()),
        out_specs=(P("row", "col", None), P("row", "col", None)),
        check_vma=False,
    )
```

```python
import functools

import jax
import jax.numpy as jnp
from jax import lax
from jax.experimental import pallas as pl
from jax.experimental.pallas import tpu as pltpu
from jax.sharding import PartitionSpec as P

eps = 1e-05
f32 = jnp.float32
bf16 = jnp.bfloat16
MESH = pl.DeviceIdType.MESH
NT = (((1,), (1,)), ((), ()))
TN = (((0,), (0,)), ((), ()))


def normalize(values, gain, shift):
    mean = jnp.mean(values, axis=-1, keepdims=True)
    centred = values - mean
    spread = jnp.mean(centred * centred, axis=-1, keepdims=True)
    return centred * lax.rsqrt(spread + eps) * gain + shift


def same_group(rows, lanes, row_size, lane_size):
    row = lax.div(lax.broadcasted_iota(jnp.int32, (rows, lanes), 0), jnp.int32(row_size))
    lane = lax.div(lax.broadcasted_iota(jnp.int32, (rows, lanes), 1), jnp.int32(lane_size))
    return row == lane


def kernel(
    R, C,
    pair_hbm, ng_hbm, ns_hbm, tw_hbm, tg_hbm, ts_hbm, tow_hbm, ag_hbm, as_hbm, aw_hbm, bw_hbm, aow_hbm,
    mid_ref, out_ref,
    pair_ref, ng_ref, ns_ref, tw_ref, tg_ref, ts_ref, tow_ref, ag_ref, as_ref, aw_ref, bw_ref, aow_ref,
    fetch_sem,
    scr, gate_scr, send_a, recv_a, send_b, recv_b, send_d, recv_d, send_bias, recv_bias, send_f, recv_f,
    sems,
):
    D = R * C
    rows, cols, width = pair_ref.shape
    hidden = tow_ref.shape[0]
    heads = bw_ref.shape[0]
    inner = aow_ref.shape[0]
    head_dim = inner // heads
    places = rows * cols
    residues = R * rows
    per = hidden // D
    lanes = per * cols
    share = cols // R
    parts, _, chunk = send_f.shape[:3]
    r, c = lax.axis_index("row"), lax.axis_index("col")
    me = r * C + c

    barrier = pltpu.get_barrier_semaphore()

    def greet(s, _):
        t = lax.rem(me + s, D)
        pl.semaphore_signal(
            barrier, inc=1, device_id=(lax.div(t, C), lax.rem(t, C)), device_id_type=MESH
        )
        return _

    lax.fori_loop(1, D, greet, 0)

    fetches = [
        pltpu.make_async_copy(source, target, fetch_sem.at[n])
        for n, (source, target) in enumerate(
            [
                (pair_hbm, pair_ref), (ng_hbm, ng_ref), (ns_hbm, ns_ref), (tw_hbm, tw_ref),
                (tg_hbm, tg_ref), (ts_hbm, ts_ref), (tow_hbm, tow_ref), (ag_hbm, ag_ref),
                (as_hbm, as_ref), (aw_hbm, aw_ref), (bw_hbm, bw_ref), (aow_hbm, aow_ref),
            ]
        )
    ]
    for fetch in fetches:
        fetch.start()
    for fetch in fetches[:4]:
        fetch.wait()

    x = pair_ref[...].astype(f32).reshape(places, width)
    normed = normalize(x, ng_ref[...], ns_ref[...]).astype(bf16)

    def spread_channels(side):
        at = 2 * hidden * side
        gate = lax.dot_general(
            tw_ref[:, at : at + hidden], normed, (((0,), (1,)), ((), ())), preferred_element_type=f32
        )
        value = lax.dot_general(
            tw_ref[:, at + hidden : at + 2 * hidden], normed, (((0,), (1,)), ((), ())),
            preferred_element_type=f32,
        )
        turned = jax.nn.sigmoid(gate) * value
        for i in range(rows):
            pieces = [
                turned[h * D : (h + 1) * D, i * cols : (i + 1) * cols] for h in range(per)
            ]
            scr[pl.ds(i, D, stride=rows), :] = jnp.concatenate(pieces, axis=1)
        send_a[side] = scr[...].astype(bf16).reshape(D, rows, lanes)

    def everywhere(source, target, send_sem, recv_sem):
        def body(s, _):
            t = lax.rem(me + s, D)
            pltpu.make_async_remote_copy(
                src_ref=source(t), dst_ref=target, send_sem=send_sem, recv_sem=recv_sem,
                device_id=(lax.div(t, C), lax.rem(t, C)), device_id_type=MESH,
            ).start()
            return _

        lax.fori_loop(1, D, body, 0)

    def along_rows(source, target, send_sem, recv_sem):
        def body(s, _):
            t = lax.rem(r + s, R)
            pltpu.make_async_remote_copy(
                src_ref=source(t), dst_ref=target, send_sem=send_sem, recv_sem=recv_sem,
                device_id=(t, c), device_id_type=MESH,
            ).start()
            return _

        lax.fori_loop(1, R, body, 0)

    def wait_bytes(ref, sem):
        pltpu.make_async_copy(ref, ref, sem).wait()

    spread_channels(1)
    pl.semaphore_wait(barrier, D - 1)
    everywhere(lambda t: send_a.at[1, t], recv_a.at[1, me], sems.at[0], sems.at[1])
    spread_channels(0)
    everywhere(lambda t: send_a.at[0, t], recv_a.at[0, me], sems.at[2], sems.at[3])
    recv_a[0, me] = send_a[0, me]
    recv_a[1, me] = send_a[1, me]
    gate_scr[...] = jax.nn.sigmoid(
        jnp.dot(normed, tw_ref[:, 4 * hidden :], preferred_element_type=f32)
    )
    for fetch in fetches[4:]:
        fetch.wait()
    wait_bytes(recv_a.at[1, pl.ds(0, D - 1)], sems.at[1])
    wait_bytes(recv_a.at[0, pl.ds(0, D - 1)], sems.at[3])

    def arrived(side, k):
        return jnp.concatenate([recv_a[side, q * C + k] for q in range(R)], axis=0)

    left = jnp.concatenate([arrived(0, k) for k in range(C)], axis=1)
    right = jnp.concatenate([arrived(1, k) for k in range(C)], axis=1)
    own_channel = jnp.concatenate([same_group(lanes, lanes, cols, cols)] * C, axis=1)
    for b in range(C):
        block = right[b * cols : (b + 1) * cols]
        block = jnp.where(own_channel, jnp.concatenate([block] * per, axis=0).astype(f32), 0.0)
        edges = lax.dot_general(left, block.astype(bf16), NT, preferred_element_type=f32)
        send_b[b] = edges.reshape(R, rows, lanes).astype(send_b.dtype)
    everywhere(
        lambda t: send_b.at[lax.rem(t, C), lax.div(t, C)], recv_b.at[me], sems.at[4], sems.at[5]
    )
    recv_b[me] = send_b[c, r]
    wait_bytes(recv_b.at[pl.ds(0, D - 1)], sems.at[5])

    def over_groups(v):
        total = v
        for h in range(1, per):
            total = total + pltpu.roll(v, h * cols, 1)
        return total

    edges = recv_b[...].astype(f32)
    mean = over_groups(jnp.sum(edges, axis=0)) * (1.0 / hidden)
    centred = edges - mean[None]
    spread = over_groups(jnp.sum(centred * centred, axis=0)) * (1.0 / hidden)
    scaled = centred * lax.rsqrt(spread + eps)[None]
    scr[...] = scaled.reshape(D * rows, lanes)
    gathered = []
    for i in range(rows):
        turned = scr[pl.ds(i, D, stride=rows), :].T
        gathered.append(
            jnp.concatenate([turned[h * cols : (h + 1) * cols] for h in range(per)], axis=1)
        )
    tri_normed = (jnp.concatenate(gathered, axis=0) * tg_ref[...] + ts_ref[...]).astype(bf16)
    update = jnp.dot(tri_normed, tow_ref[...], preferred_element_type=f32)
    x = pair_ref[...].astype(f32).reshape(places, width)
    mid = (x + gate_scr[...] * update).astype(bf16)
    mid_ref[...] = mid.reshape(rows, cols, width)

    att_in = normalize(mid.astype(f32), ag_ref[...], as_ref[...]).astype(bf16).astype(f32)
    for i in range(rows):
        gate_scr[pl.ds(i, cols, stride=rows), :] = att_in[i * cols : (i + 1) * cols]
    att_t = gate_scr[...].astype(bf16)
    send_d[...] = att_t.reshape(R, share, rows, width)
    along_rows(lambda t: send_d.at[t], recv_d.at[r], sems.at[6], sems.at[7])
    wide = heads * cols
    spread_bw = jnp.concatenate(
        [
            jnp.broadcast_to(bw_ref[...].astype(f32)[h : h + 1], (cols, width))
            for h in range(heads)
        ],
        axis=0,
    ).astype(bf16)
    products = lax.dot_general(att_t, spread_bw, NT, preferred_element_type=f32)
    products = products.reshape(cols, rows, wide)
    lane_col = lax.rem(lax.broadcasted_iota(jnp.int32, (rows, wide), 1), jnp.int32(cols))
    bias = jnp.zeros((rows, wide), f32)
    for y in range(cols):
        bias = jnp.where(lane_col == y, products[y], bias)
    send_bias[...] = bias.astype(bf16)
    everywhere(lambda t: send_bias, recv_bias.at[me], sems.at[8], sems.at[9])
    recv_d[r] = send_d[r]
    recv_bias[me] = send_bias[...]
    wait_bytes(recv_d.at[pl.ds(0, R - 1)], sems.at[7])

    columns = [recv_d[:, j].reshape(residues, width) for j in range(share)]
    own_head = same_group(wide, inner, cols, head_dim)
    projected = [jnp.dot(a, aw_ref[...], preferred_element_type=f32) for a in columns]
    wait_bytes(recv_bias.at[pl.ds(0, D - 1)], sems.at[9])
    biases = [
        jnp.concatenate([recv_bias[q * C + b] for q in range(R)], axis=0).astype(f32)
        for b in range(C)
    ]
    for j in range(share):
        proj = projected[j]
        query = (proj[:, :inner] * head_dim ** (-0.5)).astype(bf16).astype(f32)
        key = proj[:, inner : 2 * inner].astype(bf16)
        value = proj[:, 2 * inner : 3 * inner].astype(bf16)
        gate = jax.nn.sigmoid(proj[:, 3 * inner :])
        mixed = []
        for b in range(C):
            tiled = jnp.concatenate([query[b * cols : (b + 1) * cols]] * heads, axis=0)
            tiled = jnp.where(own_head, tiled, 0.0).astype(bf16)
            scores = lax.dot_general(key, tiled, NT, preferred_element_type=f32)
            scores = scores + biases[b]
            top = jnp.max(scores, axis=0, keepdims=True)
            expd = jnp.exp(scores - top)
            total = jnp.sum(expd, axis=0, keepdims=True)
            weights = (expd * (1.0 / total)).astype(bf16)
            full = lax.dot_general(weights, value, TN, preferred_element_type=f32)
            full = jnp.where(own_head, full, 0.0)
            part = full[:cols]
            for h in range(1, heads):
                part = part + full[h * cols : (h + 1) * cols]
            mixed.append(part)
        gated = (jnp.concatenate(mixed, axis=0) * gate).astype(bf16)
        part, at = j // chunk, j % chunk
        send_f[part, :, at] = gated.reshape(R, rows, inner)
        if at == chunk - 1:
            along_rows(
                lambda t, part=part: send_f.at[part, t], recv_f.at[part, r],
                sems.at[10 + 2 * part], sems.at[11 + 2 * part],
            )
            recv_f[part, r] = send_f[part, r]
    for part in range(parts):
        wait_bytes(recv_f.at[part, pl.ds(0, R - 1)], sems.at[11 + 2 * part])
        final = jnp.dot(
            recv_f[part].reshape(R * chunk * rows, inner), aow_ref[...], preferred_element_type=f32
        )
        for n in range(R * chunk):
            j = n // chunk * share + part * chunk + n % chunk
            gate_scr[pl.ds(j, rows, stride=cols), :] = final[n * rows : (n + 1) * rows]
    out = mid_ref[...].astype(f32).reshape(places, width) + gate_scr[...]
    out_ref[...] = out.astype(bf16).reshape(rows, cols, width)
    wait_bytes(recv_a.at[1, pl.ds(0, D - 1)], sems.at[0])
    wait_bytes(recv_a.at[0, pl.ds(0, D - 1)], sems.at[2])
    wait_bytes(recv_b.at[pl.ds(0, D - 1)], sems.at[4])
    wait_bytes(recv_d.at[pl.ds(0, R - 1)], sems.at[6])
    wait_bytes(recv_bias.at[pl.ds(0, D - 1)], sems.at[8])
    for part in range(parts):
        wait_bytes(recv_f.at[part, pl.ds(0, R - 1)], sems.at[10 + 2 * part])


def local(R, C, pair, ng, ns, tw, tg, ts, tow, ag, ash, aw, bw, aow):
    rows, cols, width = pair.shape
    D = R * C
    hidden = tow.shape[0]
    heads = bw.shape[1]
    parts = 2 if cols // R % 2 == 0 else 1
    inner = aow.shape[0]
    lanes = hidden // D * cols
    share = cols // R
    wide = heads * cols
    places = rows * cols
    vmem = pl.BlockSpec(memory_space=pltpu.VMEM)
    dma = pltpu.SemaphoreType.DMA
    operands = (pair, ng[None], ns[None], tw, tg[None], ts[None], tow, ag[None], ash[None], aw, bw.T, aow)
    return pl.pallas_call(
        functools.partial(kernel, R, C),
        out_shape=(
            jax.ShapeDtypeStruct(pair.shape, bf16),
            jax.ShapeDtypeStruct(pair.shape, bf16),
        ),
        in_specs=[pl.BlockSpec(memory_space=pl.ANY)] * 12,
        out_specs=(vmem, vmem),
        scratch_shapes=[pltpu.VMEM(v.shape, v.dtype) for v in operands]
        + [
            dma((12,)),
            pltpu.VMEM((D * rows, lanes), f32),
            pltpu.VMEM((places, width), f32),
            pltpu.VMEM((2, D, rows, lanes), bf16),
            pltpu.VMEM((2, D, rows, lanes), bf16),
            pltpu.VMEM((C, R, rows, lanes), bf16),
            pltpu.VMEM((D, rows, lanes), bf16),
            pltpu.VMEM((R, share, rows, width), bf16),
            pltpu.VMEM((R, share, rows, width), bf16),
            pltpu.VMEM((rows, wide), bf16),
            pltpu.VMEM((D, rows, wide), bf16),
            pltpu.VMEM((parts, R, share // parts, rows, inner), bf16),
            pltpu.VMEM((parts, R, share // parts, rows, inner), bf16),
            dma((10 + 2 * parts,)),
        ],
        compiler_params=pltpu.CompilerParams(
            collective_id=0, has_side_effects=True, vmem_limit_bytes=63 * 1024 * 1024
        ),
    )(*operands)


def solution(mesh):
    R, C = mesh.shape["row"], mesh.shape["col"]
    return jax.shard_map(
        functools.partial(local, R, C),
        mesh=mesh,
        in_specs=(P("row", "col", None), P(), P(), P(), P(), P(), P(), P(), P(), P(), P(), P()),
        out_specs=(P("row", "col", None), P("row", "col", None)),
        check_vma=False,
    )
```

```python
import functools

import jax
import jax.numpy as jnp
from jax import lax
from jax.experimental import pallas as pl
from jax.experimental.pallas import tpu as pltpu
from jax.sharding import PartitionSpec as P

eps = 1e-05
f32 = jnp.float32
bf16 = jnp.bfloat16
MESH = pl.DeviceIdType.MESH
NT = (((1,), (1,)), ((), ()))
TN = (((0,), (0,)), ((), ()))


def normalize(values, gain, shift):
    mean = jnp.mean(values, axis=-1, keepdims=True)
    centred = values - mean
    spread = jnp.mean(centred * centred, axis=-1, keepdims=True)
    return centred * lax.rsqrt(spread + eps) * gain + shift


def same_group(rows, lanes, row_size, lane_size):
    row = lax.div(lax.broadcasted_iota(jnp.int32, (rows, lanes), 0), jnp.int32(row_size))
    lane = lax.div(lax.broadcasted_iota(jnp.int32, (rows, lanes), 1), jnp.int32(lane_size))
    return row == lane


def kernel(
    R, C,
    pair_hbm, ng_hbm, ns_hbm, tw_hbm, tg_hbm, ts_hbm, tow_hbm, ag_hbm, as_hbm, aw_hbm, bw_hbm, aow_hbm,
    both_ref,
    pair_ref, ng_ref, ns_ref, tw_ref, tg_ref, ts_ref, tow_ref, ag_ref, as_ref, aw_ref, bw_ref, aow_ref,
    fetch_sem,
    scr, gate_scr, send_a, recv_a, send_b, recv_b, send_d, recv_d, send_bias, recv_bias, send_f, recv_f,
    sems,
):
    D = R * C
    rows, cols, width = pair_ref.shape
    hidden = tow_ref.shape[0]
    heads = bw_ref.shape[0]
    inner = aow_ref.shape[0]
    head_dim = inner // heads
    places = rows * cols
    residues = R * rows
    per = hidden // D
    lanes = per * cols
    share = cols // R
    parts, _, chunk = send_f.shape[:3]
    r, c = lax.axis_index("row"), lax.axis_index("col")
    me = r * C + c

    mid_ref, out_ref = both_ref.at[0], both_ref.at[1]
    barrier = pltpu.get_barrier_semaphore()

    fetches = [
        pltpu.make_async_copy(source, target, fetch_sem.at[n])
        for n, (source, target) in enumerate(
            [
                (pair_hbm, pair_ref), (ng_hbm, ng_ref), (ns_hbm, ns_ref), (tw_hbm, tw_ref),
                (tg_hbm, tg_ref), (ts_hbm, ts_ref), (tow_hbm, tow_ref), (ag_hbm, ag_ref),
                (as_hbm, as_ref), (aw_hbm, aw_ref), (bw_hbm, bw_ref), (aow_hbm, aow_ref),
            ]
        )
    ]
    for fetch in fetches:
        fetch.start()

    def greet(s, _):
        t = lax.rem(me + s, D)
        pl.semaphore_signal(
            barrier, inc=1, device_id=(lax.div(t, C), lax.rem(t, C)), device_id_type=MESH
        )
        return _

    lax.fori_loop(1, D, greet, 0)

    for fetch in fetches[:3]:
        fetch.wait()

    x = pair_ref[...].astype(f32).reshape(places, width)
    normed = normalize(x, ng_ref[...], ns_ref[...]).astype(bf16)

    fetches[3].wait()

    def spread_channels(side):
        at = 2 * hidden * side
        gate = lax.dot_general(
            tw_ref[:, at : at + hidden], normed, (((0,), (1,)), ((), ())), preferred_element_type=f32
        )
        value = lax.dot_general(
            tw_ref[:, at + hidden : at + 2 * hidden], normed, (((0,), (1,)), ((), ())),
            preferred_element_type=f32,
        )
        turned = jax.nn.sigmoid(gate) * value
        for i in range(rows):
            pieces = [
                turned[h * D : (h + 1) * D, i * cols : (i + 1) * cols] for h in range(per)
            ]
            scr[pl.ds(i, D, stride=rows), :] = jnp.concatenate(pieces, axis=1)
        send_a[side] = scr[...].astype(bf16).reshape(D, rows, lanes)

    def everywhere(source, target, send_sem, recv_sem):
        def body(s, _):
            t = lax.rem(me + s, D)
            pltpu.make_async_remote_copy(
                src_ref=source(t), dst_ref=target, send_sem=send_sem, recv_sem=recv_sem,
                device_id=(lax.div(t, C), lax.rem(t, C)), device_id_type=MESH,
            ).start()
            return _

        lax.fori_loop(1, D, body, 0)

    def along_rows(source, target, send_sem, recv_sem):
        def body(s, _):
            t = lax.rem(r + s, R)
            pltpu.make_async_remote_copy(
                src_ref=source(t), dst_ref=target, send_sem=send_sem, recv_sem=recv_sem,
                device_id=(t, c), device_id_type=MESH,
            ).start()
            return _

        lax.fori_loop(1, R, body, 0)

    def wait_bytes(ref, sem):
        pltpu.make_async_copy(ref, ref, sem).wait()

    spread_channels(1)
    pl.semaphore_wait(barrier, D - 1)
    everywhere(lambda t: send_a.at[1, t], recv_a.at[1, me], sems.at[0], sems.at[1])
    spread_channels(0)
    everywhere(lambda t: send_a.at[0, t], recv_a.at[0, me], sems.at[2], sems.at[3])
    recv_a[0, me] = send_a[0, me]
    recv_a[1, me] = send_a[1, me]
    gate_scr[...] = jax.nn.sigmoid(
        jnp.dot(normed, tw_ref[:, 4 * hidden :], preferred_element_type=f32)
    )
    for fetch in fetches[4:]:
        fetch.wait()
    wait_bytes(recv_a.at[1, pl.ds(0, D - 1)], sems.at[1])
    wait_bytes(recv_a.at[0, pl.ds(0, D - 1)], sems.at[3])

    def arrived(side, k):
        return jnp.concatenate([recv_a[side, q * C + k] for q in range(R)], axis=0)

    left = jnp.concatenate([arrived(0, k) for k in range(C)], axis=1)
    right = jnp.concatenate([arrived(1, k) for k in range(C)], axis=1)
    own_channel = jnp.concatenate([same_group(lanes, lanes, cols, cols)] * C, axis=1)
    for b in range(C):
        block = right[b * cols : (b + 1) * cols]
        block = jnp.where(own_channel, jnp.concatenate([block] * per, axis=0).astype(f32), 0.0)
        edges = lax.dot_general(left, block.astype(bf16), NT, preferred_element_type=f32)
        send_b[b] = edges.reshape(R, rows, lanes).astype(send_b.dtype)
    everywhere(
        lambda t: send_b.at[lax.rem(t, C), lax.div(t, C)], recv_b.at[me], sems.at[4], sems.at[5]
    )
    recv_b[me] = send_b[c, r]
    wait_bytes(recv_b.at[pl.ds(0, D - 1)], sems.at[5])

    def over_groups(v):
        total = v
        for h in range(1, per):
            total = total + pltpu.roll(v, h * cols, 1)
        return total

    edges = recv_b[...].astype(f32)
    mean = over_groups(jnp.sum(edges, axis=0)) * (1.0 / hidden)
    centred = edges - mean[None]
    spread = over_groups(jnp.sum(centred * centred, axis=0)) * (1.0 / hidden)
    scaled = centred * lax.rsqrt(spread + eps)[None]
    scr[...] = scaled.reshape(D * rows, lanes)
    gathered = []
    for i in range(rows):
        turned = scr[pl.ds(i, D, stride=rows), :].T
        gathered.append(
            jnp.concatenate([turned[h * cols : (h + 1) * cols] for h in range(per)], axis=1)
        )
    tri_normed = (jnp.concatenate(gathered, axis=0) * tg_ref[...] + ts_ref[...]).astype(bf16)
    update = jnp.dot(tri_normed, tow_ref[...], preferred_element_type=f32)
    x = pair_ref[...].astype(f32).reshape(places, width)
    mid = (x + gate_scr[...] * update).astype(bf16)
    mid_ref[...] = mid.reshape(rows, cols, width)

    att_in = normalize(mid.astype(f32), ag_ref[...], as_ref[...]).astype(bf16).astype(f32)
    for i in range(rows):
        gate_scr[pl.ds(i, cols, stride=rows), :] = att_in[i * cols : (i + 1) * cols]
    att_t = gate_scr[...].astype(bf16)
    send_d[...] = att_t.reshape(R, share, rows, width)
    wide = heads * cols
    spread_bw = jnp.concatenate(
        [
            jnp.broadcast_to(bw_ref[...].astype(f32)[h : h + 1], (cols, width))
            for h in range(heads)
        ],
        axis=0,
    ).astype(bf16)
    products = lax.dot_general(att_t, spread_bw, NT, preferred_element_type=f32)
    products = products.reshape(cols, rows, wide)
    lane_col = lax.rem(lax.broadcasted_iota(jnp.int32, (rows, wide), 1), jnp.int32(cols))
    bias = jnp.zeros((rows, wide), f32)
    for y in range(cols):
        bias = jnp.where(lane_col == y, products[y], bias)
    send_bias[...] = bias.astype(bf16)
    pairs = R // 2
    pair_row, odd = lax.div(r, 2), lax.rem(r, 2)
    slot = odd * C + c

    def to_pairs(s, _):
        t = lax.rem(pair_row + s, pairs)
        pltpu.make_async_remote_copy(
            src_ref=send_bias, dst_ref=recv_bias.at[slot, pair_row],
            send_sem=sems.at[8], recv_sem=sems.at[9],
            device_id=(t * 2 + odd, c), device_id_type=MESH,
        ).start()
        return _

    def to_plane(s, _):
        t = lax.rem(slot + s, 2 * C)
        pltpu.make_async_remote_copy(
            src_ref=recv_bias.at[slot], dst_ref=recv_bias.at[slot],
            send_sem=sems.at[10 + 2 * parts], recv_sem=sems.at[11 + 2 * parts],
            device_id=(pair_row * 2 + lax.div(t, C), lax.rem(t, C)), device_id_type=MESH,
        ).start()
        return _

    lax.fori_loop(1, pairs, to_pairs, 0)
    along_rows(lambda t: send_d.at[t], recv_d.at[r], sems.at[6], sems.at[7])
    recv_d[r] = send_d[r]
    recv_bias[slot, pair_row] = send_bias[...]
    wait_bytes(recv_bias.at[0, pl.ds(0, pairs - 1)], sems.at[9])
    lax.fori_loop(1, 2 * C, to_plane, 0)
    wait_bytes(recv_d.at[pl.ds(0, R - 1)], sems.at[7])

    columns = [recv_d[:, j].reshape(residues, width) for j in range(share)]
    own_head = same_group(wide, inner, cols, head_dim)
    head_mask = jnp.where(own_head, 1.0, 0.0).astype(bf16)
    projected = [jnp.dot(a, aw_ref[...], preferred_element_type=f32) for a in columns]
    wait_bytes(recv_bias.at[pl.ds(0, 2 * C - 1)], sems.at[11 + 2 * parts])
    biases = [
        jnp.concatenate([recv_bias[q % 2 * C + b, q // 2] for q in range(R)], axis=0).astype(f32)
        for b in range(C)
    ]
    for j in range(share):
        proj = projected[j]
        query = (proj[:, :inner] * head_dim ** (-0.5)).astype(bf16)
        key = proj[:, inner : 2 * inner].astype(bf16)
        value = proj[:, 2 * inner : 3 * inner].astype(bf16)
        gate = jax.nn.sigmoid(proj[:, 3 * inner :])
        mixed = []
        for b in range(C):
            tiled = jnp.concatenate([query[b * cols : (b + 1) * cols]] * heads, axis=0)
            tiled = tiled * head_mask
            scores = lax.dot_general(key, tiled, NT, preferred_element_type=f32)
            scores = scores + biases[b]
            top = jnp.max(scores, axis=0, keepdims=True)
            expd = jnp.exp(scores - top)
            total = jnp.sum(expd, axis=0, keepdims=True)
            weights = (expd * (1.0 / total)).astype(bf16)
            full = lax.dot_general(weights, value, TN, preferred_element_type=f32)
            full = jnp.where(own_head, full, 0.0)
            part = full[:cols]
            for h in range(1, heads):
                part = part + full[h * cols : (h + 1) * cols]
            mixed.append(part)
        gated = (jnp.concatenate(mixed, axis=0) * gate).astype(bf16)
        part, at = j // chunk, j % chunk
        send_f[part, :, at] = gated.reshape(R, rows, inner)
        if at == chunk - 1:
            along_rows(
                lambda t, part=part: send_f.at[part, t], recv_f.at[part, r],
                sems.at[10 + 2 * part], sems.at[11 + 2 * part],
            )
            recv_f[part, r] = send_f[part, r]
    for part in range(parts):
        wait_bytes(recv_f.at[part, pl.ds(0, R - 1)], sems.at[11 + 2 * part])
        final = jnp.dot(
            recv_f[part].reshape(R * chunk * rows, inner), aow_ref[...], preferred_element_type=f32
        )
        for n in range(R * chunk):
            j = n // chunk * share + part * chunk + n % chunk
            gate_scr[pl.ds(j, rows, stride=cols), :] = final[n * rows : (n + 1) * rows]
    out = mid_ref[...].astype(f32).reshape(places, width) + gate_scr[...]
    out_ref[...] = out.astype(bf16).reshape(rows, cols, width)
    wait_bytes(recv_a.at[1, pl.ds(0, D - 1)], sems.at[0])
    wait_bytes(recv_a.at[0, pl.ds(0, D - 1)], sems.at[2])
    wait_bytes(recv_b.at[pl.ds(0, D - 1)], sems.at[4])
    wait_bytes(recv_d.at[pl.ds(0, R - 1)], sems.at[6])
    wait_bytes(recv_bias.at[0, pl.ds(0, pairs - 1)], sems.at[8])
    wait_bytes(recv_bias.at[pl.ds(0, 2 * C - 1)], sems.at[10 + 2 * parts])
    for part in range(parts):
        wait_bytes(recv_f.at[part, pl.ds(0, R - 1)], sems.at[10 + 2 * part])


def local(R, C, pair, ng, ns, tw, tg, ts, tow, ag, ash, aw, bw, aow):
    rows, cols, width = pair.shape
    D = R * C
    hidden = tow.shape[0]
    heads = bw.shape[1]
    parts = 2 if cols // R % 2 == 0 else 1
    inner = aow.shape[0]
    lanes = hidden // D * cols
    share = cols // R
    wide = heads * cols
    places = rows * cols
    vmem = pl.BlockSpec(memory_space=pltpu.VMEM)
    dma = pltpu.SemaphoreType.DMA
    operands = (pair, ng[None], ns[None], tw, tg[None], ts[None], tow, ag[None], ash[None], aw, bw.T, aow)
    both = pl.pallas_call(
        functools.partial(kernel, R, C),
        out_shape=jax.ShapeDtypeStruct((2, *pair.shape), bf16),
        in_specs=[pl.BlockSpec(memory_space=pl.ANY)] * 12,
        out_specs=vmem,
        scratch_shapes=[pltpu.VMEM(v.shape, v.dtype) for v in operands]
        + [
            dma((12,)),
            pltpu.VMEM((D * rows, lanes), f32),
            pltpu.VMEM((places, width), f32),
            pltpu.VMEM((2, D, rows, lanes), bf16),
            pltpu.VMEM((2, D, rows, lanes), bf16),
            pltpu.VMEM((C, R, rows, lanes), bf16),
            pltpu.VMEM((D, rows, lanes), bf16),
            pltpu.VMEM((R, share, rows, width), bf16),
            pltpu.VMEM((R, share, rows, width), bf16),
            pltpu.VMEM((rows, wide), bf16),
            pltpu.VMEM((2 * C, R // 2, rows, wide), bf16),
            pltpu.VMEM((parts, R, share // parts, rows, inner), bf16),
            pltpu.VMEM((parts, R, share // parts, rows, inner), bf16),
            dma((12 + 2 * parts,)),
        ],
        compiler_params=pltpu.CompilerParams(
            collective_id=0, has_side_effects=True, vmem_limit_bytes=63 * 1024 * 1024
        ),
    )(*operands)
    return both[0], both[1]


def solution(mesh):
    R, C = mesh.shape["row"], mesh.shape["col"]
    return jax.shard_map(
        functools.partial(local, R, C),
        mesh=mesh,
        in_specs=(P("row", "col", None), P(), P(), P(), P(), P(), P(), P(), P(), P(), P(), P()),
        out_specs=(P("row", "col", None), P("row", "col", None)),
        check_vma=False,
    )
```
